256 devices in a mesh: dp: 16 (over y, x), expert: 16 (over z, core).
Axes of the slice: x: 4, y: 4, z: 8, core: 2. Of those that a mesh axis runs over, the one named last changes fastest.
Arguments:
- tokens: bfloat16 [16384, 2048], P(('dp', 'expert')), may hold values from -6 to 6
- expert_ids: int32 [16384, 10], P(('dp', 'expert')), may hold values from 0 to 255, all different within a row; in each aligned block of 64 rows (0 to 63, 64 to 127, ...) at most 3 rows name the same one
- gate_probs: float32 [16384, 10], P(('dp', 'expert')), may hold values from 0.03 to 0.3
- w_gate: bfloat16 [256, 2048, 512], P(('dp', 'expert')), may hold values from -0.125 to 0.125
- w_up: bfloat16 [256, 2048, 512], P(('dp', 'expert')), may hold values from -0.125 to 0.125
- w_down: bfloat16 [256, 512, 2048], P(('dp', 'expert')), may hold values from -0.25 to 0.25
- grad_out: bfloat16 [16384, 2048], P(('dp', 'expert')), may hold values from -6 to 6
Outputs:
- mixed: bfloat16 [16384, 2048], P(('dp', 'expert'))
- grad_tokens: bfloat16 [16384, 2048], P(('dp', 'expert'))
- grad_probs: float32 [16384, 10], P(('dp', 'expert'))
The draws below stay inside these ranges and needn't reach their ends.
Inputs may be any that keep to these rules, and one draw needn't show every extreme that they name: `expert_ids`: the 10 experts of a token differ. Among the 64 consecutive tokens of one device (aligned blocks), no expert is named more than 3 times.
All inputs are finite; a program needn't handle non-finite values.
Results may differ from the reference program's by a relative error of at most 0.0064.
Values may be sent and summed in bfloat16 or wider, within the bound.
No kernel may reach another device: no remote copies, remote signals or barrier semaphores. Data moves between devices by JAX's collectives and lax.ppermute only.
A program may use at most 128 MiB of HBM per device.

```python
import math
import jax
import jax.numpy as jnp
import numpy as np
from jax import lax

D = 2048
FF = 512
TOP = 10
TOK_DEV = 64
EXPERTS = 256
TOKENS = 16384
MOST = 3
DEVICES = 256


def block_levels(own_key, dims, pieces, smallest, high):
    loudness, own = 1.0, jax.random.fold_in(own_key, 6)
    for position, shards_of in pieces:
        steps = jnp.exp(jax.random.uniform(jax.random.fold_in(own, position), (shards_of,), jnp.float32, smallest / len(pieces), high / len(pieces)))
        loudness = loudness * jnp.repeat(steps, dims[position] // shards_of).reshape([-1 if axis == position else 1 for axis in range(len(dims))])
    return loudness


def assign_block(stream_key, own, number, rows, amount, top, reach, skew):
    ranking = jax.random.permutation(stream_key, amount)
    heavy_load, ordinary = portions_of(amount, rows * top, reach, skew, True), portions_of(amount, rows * top, reach, skew, False)
    places = jnp.arange(amount)

    def named(sizes, turn):
        used = int((sizes > 0).sum())
        fixed = max(1, used // 4)
        moved = fixed + (places - fixed + turn * (used - fixed)) % max(1, amount - fixed)
        return jnp.zeros((amount,), jnp.int32).at[ranking[jnp.where(places < fixed, places, moved)]].set(jnp.asarray(sizes, jnp.int32))

    sizes = jnp.where(number % 4 == 0, named(heavy_load, number // 4), named(ordinary, number - number // 4 - 1))
    mixed = jax.random.permutation(jax.random.fold_in(own, 3), amount)
    giver, receiver = mixed[0:amount // 2 * 2:2], mixed[1:amount // 2 * 2:2]
    slack = jnp.minimum(sizes[giver] - 1, reach - sizes[receiver]) // 2
    slack = jnp.where((giver == ranking[0]) | (receiver == ranking[0]) | (sizes[receiver] == 0), 0, jnp.maximum(slack, 0))
    moved = jax.random.randint(jax.random.fold_in(own, 4), (amount // 2,), 0, 1 << 20) % (slack + 1)
    sizes = sizes.at[giver].add(-moved).at[receiver].add(moved)
    labels = jnp.searchsorted(jnp.cumsum(sizes), jnp.arange(rows * top), side="right").astype(jnp.int32)
    grid = labels.reshape(top, rows).T
    grid = grid[jax.random.permutation(jax.random.fold_in(own, 1), rows)]
    turn = jax.random.randint(jax.random.fold_in(own, 2), (rows, 1), 0, top)
    return jnp.take_along_axis(grid, (jnp.arange(top)[None, :] + turn) % top, axis=1)


def portions_of(count, total, most, skew, full):
    portions = [(1 << 20) // math.isqrt(standing ** skew) + 1 for standing in range(1, count + 1)]
    largest = most if full else min(most, max(-(-total // count), total * portions[0] // sum(portions)))
    least = 1 if total - largest >= count - 1 else 0
    given, surplus = [largest] + [least] * (count - 1), total - largest - least * (count - 1)
    while surplus > 0:
        movable = [i for i in range(1, count) if given[i] < largest] or [i for i in range(1, count) if given[i] < most]
        whole, budget = sum([portions[i] for i in movable]), surplus
        for i in movable:
            addition = min(most - given[i], max(1, budget * portions[i] // whole), surplus)
            given[i] = given[i] + addition
            surplus = surplus - addition
    return np.array(given)


def bell_draw(key, dims, spread, reach, split=(), kind=jnp.bfloat16):
    level = block_levels(key, dims, split, -0.22, 0.18) if split else 1.0
    array = jax.random.normal(key, dims, jnp.float32) * spread * level
    return jnp.minimum(jnp.maximum(array, -reach), reach).astype(kind)


def setup_inputs(seed: int = 0) -> dict:
    key_of = jax.random.split(jax.random.key(seed), 8)
    tokens = bell_draw(key_of[0], (TOKENS, D), 1.0, 6.0, ((0, 256),))
    expert_ids_keys = jax.random.split(jax.random.fold_in(key_of[1], 1), TOKENS // TOK_DEV)
    expert_ids_turns = jax.random.permutation(jax.random.fold_in(key_of[1], 3), TOKENS // TOK_DEV)
    expert_ids = jax.vmap(lambda own, number: assign_block(jax.random.fold_in(key_of[1], 2), own, number, TOK_DEV, EXPERTS, TOP, MOST, 2))(expert_ids_keys, expert_ids_turns).reshape((TOKENS, TOP))
    gate_probs = jnp.clip(jnp.exp(math.log(0.3) - 2.3025852 * jax.random.uniform(key_of[2], (TOKENS, TOP), jnp.float32) ** block_levels(key_of[2], (TOKENS, TOP), ((0, 256),), -0.2, 0.2)), 0.03, 0.3)
    w_gate = bell_draw(key_of[3], (EXPERTS, D, FF), D ** -0.5, 0.125, ((0, 256),))
    w_up = bell_draw(key_of[4], (EXPERTS, D, FF), D ** -0.5, 0.125, ((0, 256),))
    w_down = bell_draw(key_of[5], (EXPERTS, FF, D), FF ** -0.5, 0.25, ((0, 256),))
    grad_out = bell_draw(key_of[6], (TOKENS, D), 1.0, 6.0, ((0, 256),))
    return {"tokens": tokens, "expert_ids": expert_ids, "gate_probs": gate_probs, "w_gate": w_gate, "w_up": w_up, "w_down": w_down, "grad_out": grad_out}


def expert_forward(rows, wg, wu, wd):
    pre_gate = jnp.dot(rows, wg, preferred_element_type=jnp.float32)
    pre_up = jnp.dot(rows, wu, preferred_element_type=jnp.float32)
    hidden = (jax.nn.silu(pre_gate) * pre_up).astype(jnp.bfloat16)
    return jnp.dot(hidden, wd, preferred_element_type=jnp.float32).astype(jnp.bfloat16)


def expert_backward(rows, scaled, wg, wu, wd):
    pre_gate = jnp.dot(rows, wg, preferred_element_type=jnp.float32)
    pre_up = jnp.dot(rows, wu, preferred_element_type=jnp.float32)
    sig = jax.nn.sigmoid(pre_gate)
    grad_hidden = lax.dot_general(scaled, wd, (((1,), (1,)), ((), ())), preferred_element_type=jnp.float32)
    grad_gate = (grad_hidden * pre_up * sig * (1.0 + pre_gate * (1.0 - sig))).astype(jnp.bfloat16)
    grad_up = (grad_hidden * pre_gate * sig).astype(jnp.bfloat16)
    total = lax.dot_general(grad_gate, wg, (((1,), (1,)), ((), ())), preferred_element_type=jnp.float32)
    total = total + lax.dot_general(grad_up, wu, (((1,), (1,)), ((), ())), preferred_element_type=jnp.float32)
    return total.astype(jnp.bfloat16)


def reference(tokens, expert_ids, gate_probs, w_gate, w_up, w_down, grad_out):
    count = TOKENS * TOP
    flat = expert_ids.reshape(-1)
    capacity = DEVICES * MOST
    tokens_pad = jnp.concatenate([tokens, jnp.zeros((1, D), tokens.dtype)], axis=0)
    grads_pad = jnp.concatenate([grad_out, jnp.zeros((1, D), grad_out.dtype)], axis=0)
    probs_pad = jnp.concatenate([gate_probs.reshape(-1), jnp.zeros((1,), gate_probs.dtype)], axis=0)

    def select(expert):
        found = jnp.nonzero(flat == expert, size=capacity, fill_value=count)[0].astype(jnp.int32)
        return found, (found // TOP).astype(jnp.int32)

    def forward_step(carry, expert):
        found, owner = select(expert)
        result = expert_forward(tokens_pad[owner], w_gate[expert], w_up[expert], w_down[expert])
        return carry.at[found].set(result), None

    routed_all, _ = lax.scan(forward_step, jnp.zeros((count + 1, D), jnp.bfloat16), jnp.arange(EXPERTS, dtype=jnp.int32))
    routed = routed_all[:count].reshape(TOKENS, TOP, D)
    mixed = jnp.sum(gate_probs[:, :, None] * routed.astype(jnp.float32), axis=1).astype(jnp.bfloat16)
    grad_probs = jnp.sum(grad_out[:, None, :].astype(jnp.float32) * routed.astype(jnp.float32), axis=2)

    def backward_step(carry, expert):
        found, owner = select(expert)
        scaled = (probs_pad[found][:, None] * grads_pad[owner].astype(jnp.float32)).astype(jnp.bfloat16)
        result = expert_backward(tokens_pad[owner], scaled, w_gate[expert], w_up[expert], w_down[expert])
        return carry.at[owner].add(result.astype(jnp.float32)), None

    grad_all, _ = lax.scan(backward_step, jnp.zeros((TOKENS + 1, D), jnp.float32), jnp.arange(EXPERTS, dtype=jnp.int32))
    grad_tokens = grad_all[:TOKENS].astype(jnp.bfloat16)
    return mixed, grad_tokens, grad_probs
```

```python
import jax
import jax.numpy as jnp
from jax import lax
from jax.sharding import PartitionSpec as P

BF = jnp.bfloat16
F32 = jnp.float32
LANES = 128


def reduce_bf16(x):
    return lax.reduce_precision(x, 8, 7)


def split_parts(x, count):
    parts = []
    for _ in range(count):
        head = reduce_bf16(x)
        parts.append(head.astype(BF))
        x = x - head
    return parts


def body(tokens, expert_ids, gate_probs, w_gate, w_up, w_down, grad_out):
    tok_dev, top = expert_ids.shape
    width = tokens.shape[1]
    n_data = lax.axis_size("dp")
    n_owner = lax.axis_size("expert")
    most = 3
    per = n_owner * most
    column = n_owner * tok_dev
    me = lax.axis_index("expert")
    wg, wu, wd = w_gate[0], w_up[0], w_down[0]

    pieces = [expert_ids.astype(BF)] + split_parts(gate_probs, 3)
    pieces.append(jnp.zeros((tok_dev, LANES - 4 * top), BF))
    meta = jnp.concatenate(pieces, axis=1)
    gathered = lax.all_gather(
        jnp.concatenate([tokens, meta], axis=1), "expert", axis=0, tiled=True
    )
    grads = lax.all_gather(grad_out, "expert", axis=0, tiled=True)
    rows = gathered[:, :width]
    info = gathered[:, width:].astype(F32)
    ids = info[:, :top].astype(jnp.int32)
    probs = info[:, top : 2 * top] + info[:, 2 * top : 3 * top] + info[:, 3 * top : 4 * top]

    mine = (ids % n_owner) == me
    place = jnp.where(mine, ids // n_owner, -1)
    hit = place[:, :, None] == jnp.arange(n_data, dtype=jnp.int32)[None, None, :]
    member = jnp.sum(hit.astype(F32), axis=1)
    weight = jnp.sum(jnp.where(hit, probs[:, :, None], 0.0), axis=1)
    lower = (jnp.arange(tok_dev)[:, None] > jnp.arange(tok_dev)[None, :]).astype(BF)
    rank = jnp.einsum(
        "ij,bjd->bid",
        lower,
        member.reshape(n_owner, tok_dev, n_data).astype(BF),
        preferred_element_type=F32,
    ).reshape(column, n_data)
    block = (jnp.arange(column, dtype=jnp.int32) // tok_dev)[:, None]
    slot = jnp.where(member > 0.0, block * most + rank.astype(jnp.int32), -1)
    select3 = slot.T[:, None, :] == jnp.arange(per, dtype=jnp.int32)[None, :, None]
    slot_prob = jnp.sum(jnp.where(select3, weight.T[:, None, :], 0.0), axis=2)
    select = select3.astype(BF).reshape(n_data * per, column)
    p_col = slot_prob.reshape(-1, 1)

    def route(x):
        y = lax.all_to_all(
            x.reshape(n_data, per, width), "dp", split_axis=0, concat_axis=0, tiled=True
        )
        return y.reshape(n_data * per, width)

    send_rows = jnp.dot(select, rows, preferred_element_type=F32).astype(BF)
    got_rows = route(send_rows)
    send_grads = (jnp.dot(select, grads, preferred_element_type=F32) * p_col).astype(BF)
    got_grads = route(send_grads)

    pre_gate = jnp.dot(got_rows, wg, preferred_element_type=F32)
    pre_up = jnp.dot(got_rows, wu, preferred_element_type=F32)
    sig = jax.nn.sigmoid(pre_gate)
    hidden = (pre_gate * sig * pre_up).astype(BF)
    result = jnp.dot(hidden, wd, preferred_element_type=F32).astype(BF)
    routed = route(result)

    last = (((1,), (1,)), ((), ()))
    grad_hidden = lax.dot_general(got_grads, wd, last, preferred_element_type=F32)
    grad_gate = (grad_hidden * pre_up * sig * (1.0 + pre_gate * (1.0 - sig))).astype(BF)
    grad_up = (grad_hidden * pre_gate * sig).astype(BF)
    back = lax.dot_general(grad_gate, wg, last, preferred_element_type=F32)
    back = back + lax.dot_general(grad_up, wu, last, preferred_element_type=F32)
    back = route(back.astype(BF))

    first = (((0,), (0,)), ((), ()))
    slot_dot = jnp.sum(send_grads.astype(F32) * routed.astype(F32), axis=1).reshape(n_data, per)
    slot_dot = jnp.where(slot_prob > 0.0, slot_dot / jnp.maximum(slot_prob, 1e-30), 0.0)
    by_place = jnp.sum(jnp.where(select3, slot_dot[:, :, None], 0.0), axis=1).T
    dots = jnp.sum(jnp.where(hit, by_place[:, None, :], 0.0), axis=2)
    combine = (select.astype(F32) * p_col).astype(BF)
    part = lax.dot_general(combine, routed, first, preferred_element_type=F32).astype(BF)
    tail = jnp.concatenate(
        split_parts(dots, 3) + [jnp.zeros((column, LANES - 3 * top), BF)], axis=1
    )
    summed = lax.psum_scatter(
        jnp.concatenate([part, tail], axis=1), "expert", scatter_dimension=0, tiled=True
    )
    mixed = summed[:, :width]
    ends = summed[:, width:].astype(F32)
    grad_probs = ends[:, :top] + ends[:, top : 2 * top] + ends[:, 2 * top : 3 * top]

    back_part = lax.dot_general(select, back, first, preferred_element_type=F32).astype(BF)
    grad_tokens = lax.psum_scatter(back_part, "expert", scatter_dimension=0, tiled=True)
    return (mixed, grad_tokens, grad_probs)


def solution(mesh):
    both = ("dp", "expert")
    return jax.shard_map(
        body,
        mesh=mesh,
        in_specs=(
            P(both, None),
            P(both, None),
            P(both, None),
            P(both, None, None),
            P(both, None, None),
            P(both, None, None),
            P(both, None),
        ),
        out_specs=(P(both, None), P(both, None), P(both, None)),
        check_vma=False,
    )
```

```python
import jax
import jax.numpy as jnp
from jax import lax
from jax.sharding import Mesh, PartitionSpec as P

BF = jnp.bfloat16
F32 = jnp.float32
LANES = 128
MOST = 3
PLANE = ("y", "x", "core")
FIRST = (((0,), (0,)), ((), ()))
LAST = (((1,), (1,)), ((), ()))


def shift(x, by):
    n = lax.axis_size("z")
    return lax.ppermute(x, "z", [(i, (i + by) % n) for i in range(n)])


def locate(info, first, low, count, tok_dev, top):
    n_z = lax.axis_size("z")
    n_core = lax.axis_size("core")
    n_dest = lax.axis_size("y") * lax.axis_size("x") * n_core
    n_block = info.shape[0] // (2 * tok_dev)
    info = info.astype(F32)
    ids = info[:, :top].astype(jnp.int32)
    probs = info[:, top : 2 * top] + info[:, 2 * top : 3 * top] + info[:, 3 * top : 4 * top]
    mine = (ids // n_core) % n_z == lax.axis_index("z")
    place = jnp.where(mine, ids // (n_core * n_z) * n_core + ids % n_core, -1)
    hit = place[:, :, None] == jnp.arange(n_dest, dtype=jnp.int32)[None, None, :]
    member = jnp.sum(hit.astype(F32), axis=1)
    weight = jnp.sum(jnp.where(hit, probs[:, :, None], 0.0), axis=1)
    row = jnp.arange(2 * tok_dev, dtype=jnp.int32)
    lower = (row[:, None] > row[None, :]) & (row[:, None] // tok_dev == row[None, :] // tok_dev)
    rank = jnp.einsum(
        "ij,bjd->bid",
        lower.astype(BF),
        member.reshape(n_block, 2 * tok_dev, n_dest).astype(BF),
        preferred_element_type=F32,
    ).reshape(-1, n_dest)
    row = jnp.arange(info.shape[0], dtype=jnp.int32)[:, None]
    slot = (first + row // (2 * tok_dev)) * MOST + rank.astype(jnp.int32) - low
    valid = (member > 0.0) & (slot >= 0) & (slot < count)
    code = jnp.where(valid, slot + row // tok_dev % 2 * count, -1)
    return hit, weight.T, code.T


def tokens_only(x, axis, tok_dev):
    parts = x.reshape(x.shape[:axis] + (-1, 2 * tok_dev) + x.shape[axis + 1 :])
    parts = lax.slice_in_dim(parts, 0, tok_dev, axis=axis + 1)
    return parts.reshape(x.shape[:axis] + (-1,) + x.shape[axis + 1 :])


def matches(code, count):
    return code[:, None, :] == jnp.arange(count, dtype=jnp.int32)[None, :, None]


def weighted(slot_prob, payload):
    ones = jnp.ones_like(slot_prob)
    pair = [ones, slot_prob] if payload else [slot_prob, ones]
    return jnp.concatenate(pair, axis=1).reshape(-1, 1)


def route(x):
    return lax.all_to_all(x, PLANE, split_axis=0, concat_axis=0, tiled=True)


def forward(rows, wg, wu, wd):
    pre_gate = jnp.dot(rows, wg, preferred_element_type=F32)
    pre_up = jnp.dot(rows, wu, preferred_element_type=F32)
    hidden = (pre_gate * jax.nn.sigmoid(pre_gate) * pre_up).astype(BF)
    return pre_gate, pre_up, jnp.dot(hidden, wd, preferred_element_type=F32).astype(BF)


def backward(scaled, pre_gate, pre_up, wg, wu, wd):
    sig = jax.nn.sigmoid(pre_gate)
    grad_hidden = lax.dot_general(scaled, wd, LAST, preferred_element_type=F32)
    grad_gate = (grad_hidden * pre_up * sig * (1.0 + pre_gate * (1.0 - sig))).astype(BF)
    grad_up = (grad_hidden * pre_gate * sig).astype(BF)
    back = lax.dot_general(grad_gate, wg, LAST, preferred_element_type=F32)
    back = back + lax.dot_general(grad_up, wu, LAST, preferred_element_type=F32)
    return back.astype(BF)


def expert(arrived, wg, wu, wd):
    n_dest, pair, width = arrived.shape
    half = (n_dest, pair // 2, width)
    rows = arrived[:, : pair // 2].reshape(-1, width)
    scaled = arrived[:, pair // 2 :].reshape(-1, width)
    pre_gate, pre_up, routed = forward(rows, wg, wu, wd)
    back = backward(scaled, pre_gate, pre_up, wg, wu, wd)
    return routed.reshape(half), back.reshape(half)


def token_dots(routed, scaled, slot_prob, code, hit):
    dots = jnp.sum(scaled.astype(F32) * routed.astype(F32), axis=2)
    dots = jnp.where(slot_prob > 0.0, dots / jnp.maximum(slot_prob, 1e-30), 0.0)
    by_place = jnp.sum(jnp.where(matches(code, dots.shape[1]), dots[:, :, None], 0.0), axis=1).T
    return spread_parts(jnp.sum(jnp.where(hit, by_place[:, None, :], 0.0), axis=2), 0, 3)


def spread_parts(x, first, count):
    n = x.shape[1]
    total = 0.0
    for part in range(count):
        begin = (first + part) * n
        rest = jnp.pad(x, ((0, 0), (begin, LANES - begin - n)))
        for _ in range(part):
            rest = rest - lax.reduce_precision(rest, 8, 7)
        total = total + lax.reduce_precision(rest, 8, 7)
    return total


def body(tokens, expert_ids, gate_probs, w_gate, w_up, w_down, grad_out):
    tok_dev, top = expert_ids.shape
    width = tokens.shape[1]
    n_dest = lax.axis_size("y") * lax.axis_size("x") * lax.axis_size("core")
    wg, wu, wd = w_gate[0], w_up[0], w_down[0]

    meta = jnp.pad(expert_ids.astype(F32), ((0, 0), (0, LANES - top)))
    meta = (meta + spread_parts(gate_probs, 1, 3)).astype(BF)
    own = jnp.concatenate(
        [jnp.concatenate([tokens, meta], axis=1), jnp.concatenate([grad_out, meta], axis=1)],
        axis=0,
    )

    def start(blocks, begin, low, count):
        info = jnp.concatenate([b[:, width:] for b in blocks], axis=0)
        hit, weight, code = locate(info, begin, low, count, tok_dev, top)
        match = matches(code, 2 * count)
        slot_prob = jnp.sum(jnp.where(match, weight[:, None, :], 0.0), axis=2)[:, :count]
        rows = jnp.concatenate([b[:, :width] for b in blocks], axis=0)
        select = match.astype(BF).reshape(n_dest * 2 * count, -1)
        sent = jnp.dot(select, rows, preferred_element_type=F32)
        sent = (sent * weighted(slot_prob, 1)).astype(BF)
        hit, code = tokens_only(hit, 0, tok_dev), tokens_only(code, 1, tok_dev)
        return sent.reshape(n_dest, 2 * count, width), hit, code, slot_prob

    right, left = shift(own, 1), shift(own, -1)
    blocks = [own, right, left]
    sent_near, hit_near, code_near, prob_near = start(blocks, 0, 0, 8)
    sent_near, right, left = lax.optimization_barrier((sent_near, right, left))
    got_near = route(sent_near)
    for _ in range(2):
        right, left = shift(right, 1), shift(left, -1)
        blocks += [right, left]
    blocks.append(
        jnp.concatenate([shift(right[:tok_dev], 1), shift(left[tok_dev:], -1)], axis=0)
    )
    sent_far, hit_far, code_far, prob_far = start(blocks[2:], 2, 8, 16)
    sent_far, got_near = lax.optimization_barrier((sent_far, got_near))
    got_far = route(sent_far)

    routed_far, back_far = expert(got_far, wg, wu, wd)
    back_near = jnp.concatenate(expert(got_near, wg, wu, wd), axis=1)
    ret_mixed = route(routed_far)
    ret_mixed, back_far, back_near = lax.optimization_barrier((ret_mixed, back_far, back_near))
    ret_back = route(back_far)

    def ring(part):
        half = tok_dev // 2
        right, left = shift(part[5, :half].astype(BF), 1), shift(part[5, half:].astype(BF), -1)
        right = jnp.pad(right.astype(F32), ((0, half), (0, 0))) + part[4]
        left = jnp.pad(left.astype(F32), ((half, 0), (0, 0))) + part[3]
        return shift(right.astype(BF), 1), shift(left.astype(BF), -1)

    def onward(part, right, left):
        right, left = right.astype(F32) + part[2], left.astype(F32) + part[1]
        return shift(right.astype(BF), 1), shift(left.astype(BF), -1)

    one = matches(code_far, 16).astype(F32)
    flat = (n_dest * 16, 6 * tok_dev)
    scaled = (one * prob_far[:, :, None]).astype(BF).reshape(flat)
    far = lax.dot_general(
        scaled, ret_mixed.reshape(-1, width), FIRST, preferred_element_type=F32
    )
    ends = token_dots(ret_mixed, sent_far[:, 16:], prob_far, code_far, hit_far)
    far = jnp.concatenate([far, ends], axis=1).reshape(6, tok_dev, width + LANES)
    far_mixed = far
    mixed_right, mixed_left = ring(far)
    ret_back, mixed_right, mixed_left = lax.optimization_barrier(
        (ret_back, mixed_right, mixed_left)
    )

    mixed_right, mixed_left = onward(far_mixed, mixed_right, mixed_left)
    ret_back, back_near = lax.optimization_barrier((ret_back, back_near))
    ret_near = route(back_near)
    far = lax.dot_general(
        one.astype(BF).reshape(flat),
        ret_back.reshape(-1, width),
        FIRST,
        preferred_element_type=F32,
    ).reshape(6, tok_dev, width)
    far_back = far
    back_right, back_left = onward(far, *ring(far))
    ret_near, back_right, back_left = lax.optimization_barrier((ret_near, back_right, back_left))

    one = matches(code_near, 8).astype(F32)
    flat = (n_dest * 8, 3 * tok_dev)
    scaled = (one * prob_near[:, :, None]).astype(BF).reshape(flat)
    one = one.astype(BF).reshape(flat)
    near = [
        lax.dot_general(
            select, rows.reshape(-1, width), FIRST, preferred_element_type=F32
        ).reshape(3, tok_dev, width)
        for select, rows in ((scaled, ret_near[:, :8]), (one, ret_near[:, 8:]))
    ]
    ends = token_dots(ret_near[:, :8], sent_near[:, 8:], prob_near, code_near, hit_near)
    ends = ends.reshape(3, tok_dev, LANES)

    def last(part, right, left, extra):
        right = right.astype(F32) + part[2] + extra
        left = left.astype(F32) + part[1]
        return shift(right.astype(BF), 1), shift(left.astype(BF), -1)

    right, left = last(near[1], back_right, back_left, far_back[0])
    grad_tokens = (near[1][0] + right.astype(F32) + left.astype(F32)).astype(BF)
    near_mixed = jnp.concatenate([near[0], ends], axis=2)
    right, left = last(near_mixed, mixed_right, mixed_left, far_mixed[0])
    total = near_mixed[0] + right.astype(F32) + left.astype(F32)
    mixed = total[:, :width].astype(BF)
    ends = total[:, width:]
    grad_probs = ends[:, :top] + ends[:, top : 2 * top] + ends[:, 2 * top : 3 * top]
    return (mixed, grad_tokens, grad_probs)


def solution(mesh):
    fine = Mesh(mesh.devices.reshape(4, 4, 8, 2), ("y", "x", "z", "core"))
    both = ("y", "x", "z", "core")
    return jax.shard_map(
        body,
        mesh=fine,
        in_specs=(
            P(both, None),
            P(both, None),
            P(both, None),
            P(both, None, None),
            P(both, None, None),
            P(both, None, None),
            P(both, None),
        ),
        out_specs=(P(both, None), P(both, None), P(both, None)),
        check_vma=False,
    )
```

```python
import jax
import jax.numpy as jnp
from jax import lax
from jax.experimental.layout import Layout, with_layout_constraint
from jax.sharding import Mesh, PartitionSpec as P

BF = jnp.bfloat16
F32 = jnp.float32
LANES = 128
MOST = 3
PLANE = ("y", "x", "core")
FIRST = (((0,), (0,)), ((), ()))
LAST = (((1,), (1,)), ((), ()))


def shift(x, by):
    n = lax.axis_size("z")
    return lax.ppermute(x, "z", [(i, (i + by) % n) for i in range(n)])


def locate(info, tok_dev, top):
    n_z = lax.axis_size("z")
    n_core = lax.axis_size("core")
    n_dest = lax.axis_size("y") * lax.axis_size("x") * n_core
    info = info.astype(F32)
    ids = info[:, :top].astype(jnp.int32)
    probs = info[:, top : 2 * top] + info[:, 2 * top : 3 * top] + info[:, 3 * top : 4 * top]
    mine = (ids // n_core) % n_z == lax.axis_index("z")
    place = jnp.where(mine, ids // (n_core * n_z) * n_core + ids % n_core, -1)
    hit = place[:, :, None] == jnp.arange(n_dest, dtype=jnp.int32)[None, None, :]
    member = jnp.sum(hit.astype(F32), axis=1)
    weight = jnp.sum(jnp.where(hit, probs[:, :, None], 0.0), axis=1)
    row = jnp.arange(tok_dev, dtype=jnp.int32)
    rank = jnp.einsum(
        "ij,bjd->bid",
        (row[:, None] > row[None, :]).astype(BF),
        member.reshape(-1, tok_dev, n_dest).astype(BF),
        preferred_element_type=F32,
    ).reshape(-1, n_dest)
    block = jnp.arange(info.shape[0], dtype=jnp.int32)[:, None] // tok_dev
    slot = jnp.where(member > 0.0, block * MOST + rank.astype(jnp.int32), -1)
    return hit, weight.T, slot.T


def matches(code, count):
    return code[:, None, :] == jnp.arange(count, dtype=jnp.int32)[None, :, None]


def route(x):
    return lax.all_to_all(x, PLANE, split_axis=0, concat_axis=0, tiled=True)


def token_dots(routed, scaled, slot_prob, code, hit):
    dots = jnp.sum(scaled.astype(F32) * routed.astype(F32), axis=2)
    dots = jnp.where(slot_prob > 0.0, dots / jnp.maximum(slot_prob, 1e-30), 0.0)
    by_place = jnp.sum(jnp.where(matches(code, dots.shape[1]), dots[:, :, None], 0.0), axis=1).T
    return spread_parts(jnp.sum(jnp.where(hit, by_place[:, None, :], 0.0), axis=2), 0, 3)


def spread_parts(x, first, count):
    n = x.shape[1]
    total = 0.0
    for part in range(count):
        begin = (first + part) * n
        rest = jnp.pad(x, ((0, 0), (begin, LANES - begin - n)))
        for _ in range(part):
            rest = rest - lax.reduce_precision(rest, 8, 7)
        total = total + lax.reduce_precision(rest, 8, 7)
    return total


def body(tokens, expert_ids, gate_probs, w_gate, w_up, w_down, grad_out):
    tok_dev, top = expert_ids.shape
    width = tokens.shape[1]
    n_dest = lax.axis_size("y") * lax.axis_size("x") * lax.axis_size("core")
    wg, wu, wd = w_gate[0], w_up[0], w_down[0]

    meta = jnp.pad(expert_ids.astype(F32), ((0, 0), (0, LANES - top)))
    meta = (meta + spread_parts(gate_probs, 1, 3)).astype(BF)
    def pick(match, rows):
        select = match.astype(BF).reshape(-1, rows.shape[0])
        return jnp.dot(select, rows, preferred_element_type=F32)

    def matrix(match, slot_prob):
        match = match.astype(F32) if slot_prob is None else match * slot_prob[:, :, None]
        return match.astype(BF).reshape(-1, match.shape[2])

    def slot_weights(match, weight):
        return jnp.sum(jnp.where(match, weight[:, None, :], 0.0), axis=2)

    def ends_meet(right, left):
        half = tok_dev // 2
        return jnp.concatenate([shift(right[:half], 1), shift(left[half:], -1)], axis=0)

    def stack(blocks):
        rows = jnp.concatenate([b[:, :width] for b in blocks], axis=0)
        return with_layout_constraint(rows, Layout(major_to_minor=(0, 1)))

    own = jnp.concatenate([tokens, meta], axis=1)
    right, left = shift(own, 1), shift(own, -1)
    right, left, meta = lax.optimization_barrier((right, left, meta))
    blocks = [own, right, left]
    right, left = shift(right, 1), shift(left, -1)
    far_meta = shift(meta, 4)
    blocks += [right, left]
    right, left = shift(right, 1), shift(left, -1)
    blocks += [right, left]
    info = jnp.concatenate([b[:, width:] for b in blocks] + [far_meta], axis=0)
    hit, weight, slot = locate(info, tok_dev, top)
    match = matches(slot, 24)
    prob = slot_weights(match, weight)
    right, left, grad_own = lax.optimization_barrier((right, left, grad_out))
    blocks.append(ends_meet(right[:, :width], left[:, :width]))
    sent = pick(match, stack(blocks)).astype(BF)
    got_rows = route(sent.reshape(n_dest, 24, width))

    right, left = shift(grad_own, 1), shift(grad_own, -1)
    blocks = [grad_own, right, left]
    for _ in range(2):
        right, left = shift(right, 1), shift(left, -1)
        blocks += [right, left]
    blocks.append(ends_meet(right, left))
    sent_grads = pick(match, stack(blocks)) * prob.reshape(-1, 1)
    sent_grads = sent_grads.astype(BF).reshape(n_dest, 24, width)
    prob_near, prob_far = prob[:, :8], prob[:, 8:]
    slot_near, slot_far = slot[:, : 3 * tok_dev], slot[:, 2 * tok_dev :]
    hit_near, hit_far = hit[: 3 * tok_dev], hit[2 * tok_dev :]
    far_mixed_matrix = matrix(matches(slot_far - 8, 16), prob_far)
    far_back_matrix = matrix(matches(slot_far - 8, 16), None)
    pair_prob = jnp.concatenate([prob_near, prob_near], axis=1)
    slot_near = jnp.where(slot_near < 8, slot_near, -1)
    near_mixed_matrix = matrix(matches(slot_near, 16), pair_prob)
    near_back_matrix = matrix(matches(jnp.where(slot_near >= 0, slot_near + 8, -1), 16), None)
    sent_grads, got_rows = lax.optimization_barrier((sent_grads, got_rows))
    got_grads = route(sent_grads)

    rows = got_rows.reshape(-1, width)
    pre_gate = jnp.dot(rows, wg, preferred_element_type=F32)
    pre_up = jnp.dot(rows, wu, preferred_element_type=F32)
    sig = jax.nn.sigmoid(pre_gate)
    hidden = (pre_gate * sig * pre_up).astype(BF).reshape(n_dest, 24, -1)

    def down(hidden):
        hidden = hidden.reshape(-1, wd.shape[0])
        return jnp.dot(hidden, wd, preferred_element_type=F32).astype(BF)

    def rise(grad_gate, grad_up):
        grad_gate = grad_gate.reshape(-1, wd.shape[0])
        grad_up = grad_up.reshape(-1, wd.shape[0])
        back = lax.dot_general(grad_gate, wg, LAST, preferred_element_type=F32)
        back = back + lax.dot_general(grad_up, wu, LAST, preferred_element_type=F32)
        return back.astype(BF)

    half = (n_dest, 16, width)
    routed_far, routed_near = down(hidden[:, 8:]), down(hidden[:, :8])
    (
        got_grads,
        routed_far,
        routed_near,
        far_mixed_matrix,
        far_back_matrix,
        near_mixed_matrix,
        near_back_matrix,
    ) = lax.optimization_barrier(
        (
            got_grads,
            routed_far,
            routed_near,
            far_mixed_matrix,
            far_back_matrix,
            near_mixed_matrix,
            near_back_matrix,
        )
    )
    ret_mixed = route(routed_far.reshape(half))
    grad_hidden = lax.dot_general(
        got_grads.reshape(-1, width), wd, LAST, preferred_element_type=F32
    )
    grad_gate = (grad_hidden * pre_up * sig * (1.0 + pre_gate * (1.0 - sig))).astype(BF)
    grad_up = (grad_hidden * pre_gate * sig).astype(BF)
    grad_gate = grad_gate.reshape(n_dest, 24, -1)
    grad_up = grad_up.reshape(n_dest, 24, -1)
    back_far = rise(grad_gate[:, 8:], grad_up[:, 8:])
    back_near = rise(grad_gate[:, :8], grad_up[:, :8])
    back_near = jnp.concatenate(
        [routed_near.reshape(n_dest, 8, width), back_near.reshape(n_dest, 8, width)], axis=1
    )
    ret_mixed, back_far, back_near = lax.optimization_barrier((ret_mixed, back_far, back_near))
    ret_back = route(back_far.reshape(half))

    def gather_sums(select, ret, blocks):
        part = lax.dot_general(
            select, ret.reshape(-1, width), FIRST, preferred_element_type=F32
        )
        return part.reshape(blocks, tok_dev, width)

    def ring(part):
        half = tok_dev // 2
        right, left = shift(part[5, :half].astype(BF), 1), shift(part[5, half:].astype(BF), -1)
        right = jnp.pad(right.astype(F32), ((0, half), (0, 0))) + part[4]
        left = jnp.pad(left.astype(F32), ((half, 0), (0, 0))) + part[3]
        return shift(right.astype(BF), 1), shift(left.astype(BF), -1)

    def onward(part, right, left):
        right, left = right.astype(F32) + part[2], left.astype(F32) + part[1]
        return shift(right.astype(BF), 1), shift(left.astype(BF), -1)

    far = gather_sums(far_mixed_matrix, ret_mixed, 6)
    ends = token_dots(ret_mixed, sent_grads[:, 8:], prob_far, slot_far - 8, hit_far)
    far = jnp.concatenate([far, ends.reshape(6, tok_dev, LANES)], axis=2)
    far_mixed = far
    mixed_right, mixed_left = ring(far)
    ret_back, mixed_right, mixed_left = lax.optimization_barrier(
        (ret_back, mixed_right, mixed_left)
    )

    mixed_right, mixed_left = onward(far_mixed, mixed_right, mixed_left)
    ret_back, back_near = lax.optimization_barrier((ret_back, back_near))
    ret_near = route(back_near)
    far = gather_sums(far_back_matrix, ret_back, 6)
    far_back = far
    back_right, back_left = onward(far, *ring(far))
    ret_near, back_right, back_left = lax.optimization_barrier((ret_near, back_right, back_left))

    near_mixed = gather_sums(near_mixed_matrix, ret_near, 3)
    near_back = gather_sums(near_back_matrix, ret_near, 3)
    ends = token_dots(ret_near[:, :8], sent_grads[:, :8], prob_near, slot_near, hit_near)
    ends = ends.reshape(3, tok_dev, LANES)

    def beside(at, mixed, back):
        rows = near_mixed[at] + mixed[:, :width], near_back[at] + back
        return jnp.concatenate(rows + (ends[at] + mixed[:, width:],), axis=1)

    right = beside(
        2, mixed_right.astype(F32) + far_mixed[0], back_right.astype(F32) + far_back[0]
    )
    left = beside(1, mixed_left.astype(F32), back_left.astype(F32))
    total = shift(right.astype(BF), 1).astype(F32) + shift(left.astype(BF), -1).astype(F32)
    mixed = (total[:, :width] + near_mixed[0]).astype(BF)
    grad_tokens = (total[:, width : 2 * width] + near_back[0]).astype(BF)
    ends = total[:, 2 * width :] + ends[0]
    grad_probs = ends[:, :top] + ends[:, top : 2 * top] + ends[:, 2 * top : 3 * top]
    return (mixed, grad_tokens, grad_probs)


def solution(mesh):
    fine = Mesh(mesh.devices.reshape(4, 4, 8, 2), ("y", "x", "z", "core"))
    both = ("y", "x", "z", "core")
    return jax.shard_map(
        body,
        mesh=fine,
        in_specs=(
            P(both, None),
            P(both, None),
            P(both, None),
            P(both, None, None),
            P(both, None, None),
            P(both, None, None),
            P(both, None),
        ),
        out_specs=(P(both, None), P(both, None), P(both, None)),
        check_vma=False,
    )
```

```python
import jax
import jax.numpy as jnp
from jax import lax
from jax.experimental.layout import Layout, with_layout_constraint
from jax.sharding import Mesh, PartitionSpec as P

BF = jnp.bfloat16
F32 = jnp.float32
LANES = 128
MOST = 3
PLANE = ("y", "x", "core")
FIRST = (((0,), (0,)), ((), ()))
LAST = (((1,), (1,)), ((), ()))


def shift(x, by):
    n = lax.axis_size("z")
    return lax.ppermute(x, "z", [(i, (i + by) % n) for i in range(n)])


def locate(info, tok_dev, top):
    n_z = lax.axis_size("z")
    n_core = lax.axis_size("core")
    n_dest = lax.axis_size("y") * lax.axis_size("x") * n_core
    info = info.astype(F32)
    ids = info[:, :top].astype(jnp.int32)
    probs = info[:, top : 2 * top] + info[:, 2 * top : 3 * top] + info[:, 3 * top : 4 * top]
    mine = (ids // n_core) % n_z == lax.axis_index("z")
    place = jnp.where(mine, ids // (n_core * n_z) * n_core + ids % n_core, -1)
    hit = place[:, :, None] == jnp.arange(n_dest, dtype=jnp.int32)[None, None, :]
    member = jnp.sum(hit.astype(F32), axis=1)
    weight = jnp.sum(jnp.where(hit, probs[:, :, None], 0.0), axis=1)
    row = jnp.arange(tok_dev, dtype=jnp.int32)
    rank = jnp.einsum(
        "ij,bjd->bid",
        (row[:, None] > row[None, :]).astype(BF),
        member.reshape(-1, tok_dev, n_dest).astype(BF),
        preferred_element_type=F32,
    ).reshape(-1, n_dest)
    block = jnp.arange(info.shape[0], dtype=jnp.int32)[:, None] // tok_dev
    slot = jnp.where(member > 0.0, block * MOST + rank.astype(jnp.int32), -1)
    return hit, weight.T, slot.T


def matches(code, count):
    return code[:, None, :] == jnp.arange(count, dtype=jnp.int32)[None, :, None]


def route(x):
    return lax.all_to_all(x, PLANE, split_axis=0, concat_axis=0, tiled=True)


def token_dots(routed, scaled, slot_prob, code, hit):
    dots = jnp.sum(scaled.astype(F32) * routed.astype(F32), axis=2)
    dots = jnp.where(slot_prob > 0.0, dots / jnp.maximum(slot_prob, 1e-30), 0.0)
    by_place = jnp.sum(jnp.where(matches(code, dots.shape[1]), dots[:, :, None], 0.0), axis=1).T
    return spread_parts(jnp.sum(jnp.where(hit, by_place[:, None, :], 0.0), axis=2), 0, 3)


def spread_parts(x, first, count):
    n = x.shape[1]
    total = 0.0
    for part in range(count):
        begin = (first + part) * n
        rest = jnp.pad(x, ((0, 0), (begin, LANES - begin - n)))
        for _ in range(part):
            rest = rest - lax.reduce_precision(rest, 8, 7)
        total = total + lax.reduce_precision(rest, 8, 7)
    return total


def body(tokens, expert_ids, gate_probs, w_gate, w_up, w_down, grad_out):
    tok_dev, top = expert_ids.shape
    width = tokens.shape[1]
    n_dest = lax.axis_size("y") * lax.axis_size("x") * lax.axis_size("core")
    wg, wu, wd = w_gate[0], w_up[0], w_down[0]

    meta = jnp.pad(expert_ids.astype(F32), ((0, 0), (0, LANES - top)))
    meta = (meta + spread_parts(gate_probs, 1, 3)).astype(BF)
    def matrix(match, slot_prob):
        match = match.astype(F32) if slot_prob is None else match * slot_prob[:, :, None]
        return match.astype(BF).reshape(-1, match.shape[2])

    def slot_weights(match, weight):
        return jnp.sum(jnp.where(match, weight[:, None, :], 0.0), axis=2)

    def ends_meet(right, left):
        half = tok_dev // 2
        return jnp.concatenate([shift(right[:half], 1), shift(left[half:], -1)], axis=0)

    def stack(blocks):
        rows = jnp.concatenate([b[:, :width] for b in blocks], axis=0)
        return with_layout_constraint(rows, Layout(major_to_minor=(0, 1)))

    own = jnp.concatenate([tokens, meta], axis=1)
    right, left = shift(own, 1), shift(own, -1)
    blocks = [own, right, left]
    right, left = shift(right, 1), shift(left, -1)
    right, left, meta = lax.optimization_barrier((right, left, meta))
    far_meta = shift(meta, 4)
    blocks += [right, left]
    right, left = shift(right, 1), shift(left, -1)
    blocks += [right, left]
    info = jnp.concatenate([b[:, width:] for b in blocks] + [far_meta], axis=0)
    hit, weight, slot = locate(info, tok_dev, top)
    match = matches(slot, 24)
    prob = slot_weights(match, weight)
    select = lax.optimization_barrier(matrix(match, None))
    right, left, grad_own = lax.optimization_barrier((right, left, grad_out))
    blocks.append(ends_meet(right[:, :width], left[:, :width]))
    sent = jnp.dot(select, stack(blocks), preferred_element_type=F32).astype(BF)
    got_rows = route(sent.reshape(n_dest, 24, width))

    right, left = shift(grad_own, 1), shift(grad_own, -1)
    blocks = [grad_own, right, left]
    for _ in range(2):
        right, left = shift(right, 1), shift(left, -1)
        blocks += [right, left]
    blocks.append(ends_meet(right, left))
    sent_grads = jnp.dot(select, stack(blocks), preferred_element_type=F32)
    sent_grads = sent_grads * prob.reshape(-1, 1)
    sent_grads = sent_grads.astype(BF).reshape(n_dest, 24, width)
    prob_near, prob_far = prob[:, :8], prob[:, 8:]
    slot_near, slot_far = slot[:, : 3 * tok_dev], slot[:, 2 * tok_dev :]
    hit_near, hit_far = hit[: 3 * tok_dev], hit[2 * tok_dev :]
    far_mixed_matrix = matrix(matches(slot_far - 8, 16), prob_far)
    far_back_matrix = matrix(matches(slot_far - 8, 16), None)
    pair_prob = jnp.concatenate([prob_near, prob_near], axis=1)
    slot_near = jnp.where(slot_near < 8, slot_near, -1)
    near_mixed = matrix(matches(slot_near, 16), pair_prob)
    near_back = matrix(matches(jnp.where(slot_near >= 0, slot_near + 8, -1), 16), None)
    near_matrix = jnp.concatenate([near_mixed[:, tok_dev:], near_back[:, tok_dev:]], axis=1)
    own_matrix = jnp.concatenate([near_mixed[:, :tok_dev], near_back[:, :tok_dev]], axis=1)
    sent_grads, got_rows = lax.optimization_barrier((sent_grads, got_rows))
    got_grads = route(sent_grads)

    rows = got_rows.reshape(-1, width)
    pre_gate = jnp.dot(rows, wg, preferred_element_type=F32)
    pre_up = jnp.dot(rows, wu, preferred_element_type=F32)
    sig = jax.nn.sigmoid(pre_gate)
    hidden = (pre_gate * sig * pre_up).astype(BF).reshape(n_dest, 24, -1)

    def down(hidden):
        hidden = hidden.reshape(-1, wd.shape[0])
        return jnp.dot(hidden, wd, preferred_element_type=F32).astype(BF)

    def rise(grad_gate, grad_up):
        grad_gate = grad_gate.reshape(-1, wd.shape[0])
        grad_up = grad_up.reshape(-1, wd.shape[0])
        back = lax.dot_general(grad_gate, wg, LAST, preferred_element_type=F32)
        back = back + lax.dot_general(grad_up, wu, LAST, preferred_element_type=F32)
        return back.astype(BF)

    half = (n_dest, 16, width)
    routed_far, routed_near = down(hidden[:, 8:]), down(hidden[:, :8])
    (
        got_grads,
        routed_far,
        routed_near,
        far_mixed_matrix,
        far_back_matrix,
        near_matrix,
        own_matrix,
    ) = lax.optimization_barrier(
        (
            got_grads,
            routed_far,
            routed_near,
            far_mixed_matrix,
            far_back_matrix,
            near_matrix,
            own_matrix,
        )
    )
    ret_mixed = route(routed_far.reshape(half))
    grad_hidden = lax.dot_general(
        got_grads.reshape(-1, width), wd, LAST, preferred_element_type=F32
    )
    grad_gate = (grad_hidden * pre_up * sig * (1.0 + pre_gate * (1.0 - sig))).astype(BF)
    grad_up = (grad_hidden * pre_gate * sig).astype(BF)
    grad_gate = grad_gate.reshape(n_dest, 24, -1)
    grad_up = grad_up.reshape(n_dest, 24, -1)
    back_far = rise(grad_gate[:, 8:], grad_up[:, 8:])
    back_near = rise(grad_gate[:, :8], grad_up[:, :8])
    back_near = jnp.concatenate(
        [routed_near.reshape(n_dest, 8, width), back_near.reshape(n_dest, 8, width)], axis=1
    )
    ret_mixed, back_far, back_near = lax.optimization_barrier((ret_mixed, back_far, back_near))
    ret_back = route(back_far.reshape(half))

    def gather_sums(select, ret, blocks):
        part = lax.dot_general(
            select, ret.reshape(-1, width), FIRST, preferred_element_type=F32
        )
        return part.reshape(blocks, tok_dev, width)

    def ring(part):
        half = tok_dev // 2
        right, left = shift(part[5, :half].astype(BF), 1), shift(part[5, half:].astype(BF), -1)
        right = jnp.pad(right.astype(F32), ((0, half), (0, 0))) + part[4]
        left = jnp.pad(left.astype(F32), ((half, 0), (0, 0))) + part[3]
        return shift(right.astype(BF), 1), shift(left.astype(BF), -1)

    def onward(part, right, left):
        right, left = right.astype(F32) + part[2], left.astype(F32) + part[1]
        return shift(right.astype(BF), 1), shift(left.astype(BF), -1)

    far = gather_sums(far_mixed_matrix, ret_mixed, 6)
    ends = token_dots(ret_mixed, sent_grads[:, 8:], prob_far, slot_far - 8, hit_far)
    far = jnp.concatenate([far, ends.reshape(6, tok_dev, LANES)], axis=2)
    far_mixed = far
    mixed_right, mixed_left = ring(far)
    ret_back, mixed_right, mixed_left = lax.optimization_barrier(
        (ret_back, mixed_right, mixed_left)
    )

    mixed_right, mixed_left = onward(far_mixed, mixed_right, mixed_left)
    ret_back, back_near = lax.optimization_barrier((ret_back, back_near))
    ret_near = route(back_near)
    far = gather_sums(far_back_matrix, ret_back, 6)
    far_back = far
    back_right, back_left = onward(far, *ring(far))
    ret_near, back_right, back_left = lax.optimization_barrier((ret_near, back_right, back_left))

    sides = gather_sums(near_matrix, ret_near, 4)
    here = gather_sums(own_matrix, ret_near, 2)
    ends = token_dots(ret_near[:, :8], sent_grads[:, :8], prob_near, slot_near, hit_near)
    ends = ends.reshape(3, tok_dev, LANES)

    def beside(at, mixed, back):
        rows = sides[at - 1] + mixed[:, :width], sides[at + 1] + back
        return jnp.concatenate(rows + (ends[at] + mixed[:, width:],), axis=1)

    right = beside(
        2, mixed_right.astype(F32) + far_mixed[0], back_right.astype(F32) + far_back[0]
    )
    left = beside(1, mixed_left.astype(F32), back_left.astype(F32))
    total = shift(right.astype(BF), 1).astype(F32) + shift(left.astype(BF), -1).astype(F32)
    mixed = (total[:, :width] + here[0]).astype(BF)
    grad_tokens = (total[:, width : 2 * width] + here[1]).astype(BF)
    ends = total[:, 2 * width :] + ends[0]
    grad_probs = ends[:, :top] + ends[:, top : 2 * top] + ends[:, 2 * top : 3 * top]
    return (mixed, grad_tokens, grad_probs)


def solution(mesh):
    fine = Mesh(mesh.devices.reshape(4, 4, 8, 2), ("y", "x", "z", "core"))
    both = ("y", "x", "z", "core")
    return jax.shard_map(
        body,
        mesh=fine,
        in_specs=(
            P(both, None),
            P(both, None),
            P(both, None),
            P(both, None, None),
            P(both, None, None),
            P(both, None, None),
            P(both, None),
        ),
        out_specs=(P(both, None), P(both, None), P(both, None)),
        check_vma=False,
    )
```

```python
import jax
import jax.numpy as jnp
from jax import lax
from jax.experimental.layout import Layout, with_layout_constraint
from jax.sharding import Mesh, PartitionSpec as P

BF = jnp.bfloat16
F32 = jnp.float32
LANES = 128
MOST = 3
PLANE = ("y", "x", "core")
FIRST = (((0,), (0,)), ((), ()))
LAST = (((1,), (1,)), ((), ()))


def shift(x, by):
    n = lax.axis_size("z")
    return lax.ppermute(x, "z", [(i, (i + by) % n) for i in range(n)])


def locate(info, tok_dev, top):
    n_z = lax.axis_size("z")
    n_core = lax.axis_size("core")
    n_dest = lax.axis_size("y") * lax.axis_size("x") * n_core
    info = info.astype(F32)
    ids = info[:, :top].astype(jnp.int32)
    probs = info[:, top : 2 * top] + info[:, 2 * top : 3 * top] + info[:, 3 * top : 4 * top]
    mine = (ids // n_core) % n_z == lax.axis_index("z")
    place = jnp.where(mine, ids // (n_core * n_z) * n_core + ids % n_core, -1)
    hit = place[:, :, None] == jnp.arange(n_dest, dtype=jnp.int32)[None, None, :]
    member = jnp.sum(hit.astype(F32), axis=1)
    weight = jnp.sum(jnp.where(hit, probs[:, :, None], 0.0), axis=1)
    row = jnp.arange(tok_dev, dtype=jnp.int32)
    rank = jnp.einsum(
        "ij,bjd->bid",
        (row[:, None] > row[None, :]).astype(BF),
        member.reshape(-1, tok_dev, n_dest).astype(BF),
        preferred_element_type=F32,
    ).reshape(-1, n_dest)
    block = jnp.arange(info.shape[0], dtype=jnp.int32)[:, None] // tok_dev
    slot = jnp.where(member > 0.0, block * MOST + rank.astype(jnp.int32), -1)
    return hit, weight.T, slot.T


def matches(code, count):
    return code[:, None, :] == jnp.arange(count, dtype=jnp.int32)[None, :, None]


def route(x):
    return lax.all_to_all(x, PLANE, split_axis=0, concat_axis=0, tiled=True)


def token_dots(routed, scaled, slot_prob, code, hit):
    dots = jnp.sum(scaled.astype(F32) * routed.astype(F32), axis=2)
    dots = jnp.where(slot_prob > 0.0, dots / jnp.maximum(slot_prob, 1e-30), 0.0)
    by_place = jnp.sum(jnp.where(matches(code, dots.shape[1]), dots[:, :, None], 0.0), axis=1).T
    return spread_parts(jnp.sum(jnp.where(hit, by_place[:, None, :], 0.0), axis=2), 0, 3)


def spread_parts(x, first, count):
    n = x.shape[1]
    total = 0.0
    for part in range(count):
        begin = (first + part) * n
        rest = jnp.pad(x, ((0, 0), (begin, LANES - begin - n)))
        for _ in range(part):
            rest = rest - lax.reduce_precision(rest, 8, 7)
        total = total + lax.reduce_precision(rest, 8, 7)
    return total


def body(tokens, expert_ids, gate_probs, w_gate, w_up, w_down, grad_out):
    tok_dev, top = expert_ids.shape
    width = tokens.shape[1]
    n_dest = lax.axis_size("y") * lax.axis_size("x") * lax.axis_size("core")
    wg, wu, wd = w_gate[0], w_up[0], w_down[0]

    meta = jnp.pad(expert_ids.astype(F32), ((0, 0), (0, LANES - top)))
    meta = (meta + spread_parts(gate_probs, 1, 3)).astype(BF)
    def matrix(match, slot_prob):
        match = match.astype(F32) if slot_prob is None else match * slot_prob[:, :, None]
        return match.astype(BF).reshape(-1, match.shape[2])

    def slot_weights(match, weight):
        return jnp.sum(jnp.where(match, weight[:, None, :], 0.0), axis=2)

    def ends_meet(right, left):
        half = tok_dev // 2
        return [shift(right[:half], 1), shift(left[half:], -1)]

    def stack(blocks):
        rows = jnp.concatenate([b[:, :width] for b in blocks], axis=0)
        return with_layout_constraint(rows, Layout(major_to_minor=(0, 1)))

    own = jnp.concatenate([tokens, meta], axis=1)
    right, left = shift(own, 1), shift(own, -1)
    blocks = [own, right, left]
    right, left = shift(right, 1), shift(left, -1)
    right, left, meta = lax.optimization_barrier((right, left, meta))
    far_meta = shift(meta, 4)
    blocks += [right, left]
    right, left = shift(right, 1), shift(left, -1)
    blocks += [right, left]
    info = jnp.concatenate([b[:, width:] for b in blocks] + [far_meta], axis=0)
    hit, weight, slot = locate(info, tok_dev, top)
    match = matches(slot, 24)
    prob = slot_weights(match, weight)
    select = lax.optimization_barrier(matrix(match, None))
    right, left, grad_own = lax.optimization_barrier((right, left, grad_out))
    blocks += ends_meet(right[:, :width], left[:, :width])
    sent = jnp.dot(select, stack(blocks), preferred_element_type=F32).astype(BF)
    got_rows = route(sent.reshape(n_dest, 24, width))

    right, left = shift(grad_own, 1), shift(grad_own, -1)
    blocks = [grad_own, right, left]
    for _ in range(2):
        right, left = shift(right, 1), shift(left, -1)
        blocks += [right, left]
    blocks += ends_meet(right, left)
    sent_grads = jnp.dot(select, stack(blocks), preferred_element_type=F32)
    sent_grads = sent_grads * prob.reshape(-1, 1)
    sent_grads = sent_grads.astype(BF).reshape(n_dest, 24, width)
    prob_near, prob_far = prob[:, :8], prob[:, 8:]
    slot_near, slot_far = slot[:, : 3 * tok_dev], slot[:, 2 * tok_dev :]
    hit_near, hit_far = hit[: 3 * tok_dev], hit[2 * tok_dev :]
    far_mixed_matrix = matrix(matches(slot_far - 8, 16), prob_far)
    far_back_matrix = matrix(matches(slot_far - 8, 16), None)
    pair_prob = jnp.concatenate([prob_near, prob_near], axis=1)
    slot_near = jnp.where(slot_near < 8, slot_near, -1)
    near_mixed = matrix(matches(slot_near, 16), pair_prob)
    near_back = matrix(matches(jnp.where(slot_near >= 0, slot_near + 8, -1), 16), None)
    near_matrix = jnp.concatenate([near_mixed[:, tok_dev:], near_back[:, tok_dev:]], axis=1)
    own_matrix = jnp.concatenate([near_mixed[:, :tok_dev], near_back[:, :tok_dev]], axis=1)
    sent_grads, got_rows = lax.optimization_barrier((sent_grads, got_rows))
    got_grads = route(sent_grads)

    rows = got_rows.reshape(-1, width)
    pre_gate = jnp.dot(rows, wg, preferred_element_type=F32)
    pre_up = jnp.dot(rows, wu, preferred_element_type=F32)
    sig = jax.nn.sigmoid(pre_gate)
    hidden = (pre_gate * sig * pre_up).astype(BF).reshape(n_dest, 24, -1)

    def down(hidden):
        hidden = hidden.reshape(-1, wd.shape[0])
        return jnp.dot(hidden, wd, preferred_element_type=F32).astype(BF)

    def rise(grad_gate, grad_up):
        grad_gate = grad_gate.reshape(-1, wd.shape[0])
        grad_up = grad_up.reshape(-1, wd.shape[0])
        back = lax.dot_general(grad_gate, wg, LAST, preferred_element_type=F32)
        back = back + lax.dot_general(grad_up, wu, LAST, preferred_element_type=F32)
        return back.astype(BF)

    half = (n_dest, 16, width)
    routed_far, routed_near = down(hidden[:, 8:]), down(hidden[:, :8])
    (
        got_grads,
        routed_far,
        routed_near,
        far_mixed_matrix,
        far_back_matrix,
        near_matrix,
        own_matrix,
    ) = lax.optimization_barrier(
        (
            got_grads,
            routed_far,
            routed_near,
            far_mixed_matrix,
            far_back_matrix,
            near_matrix,
            own_matrix,
        )
    )
    ret_mixed = route(routed_far.reshape(half))
    grad_hidden = lax.dot_general(
        got_grads.reshape(-1, width), wd, LAST, preferred_element_type=F32
    )
    grad_gate = (grad_hidden * pre_up * sig * (1.0 + pre_gate * (1.0 - sig))).astype(BF)
    grad_up = (grad_hidden * pre_gate * sig).astype(BF)
    grad_gate = grad_gate.reshape(n_dest, 24, -1)
    grad_up = grad_up.reshape(n_dest, 24, -1)
    back_far = rise(grad_gate[:, 8:], grad_up[:, 8:])
    back_near = rise(grad_gate[:, :8], grad_up[:, :8])
    back_near = jnp.concatenate(
        [routed_near.reshape(n_dest, 8, width), back_near.reshape(n_dest, 8, width)], axis=1
    )
    ret_mixed, back_far, back_near = lax.optimization_barrier((ret_mixed, back_far, back_near))
    ret_back = route(back_far.reshape(half))

    def gather_sums(select, ret, blocks):
        part = lax.dot_general(
            select, ret.reshape(-1, width), FIRST, preferred_element_type=F32
        )
        return part.reshape(blocks, tok_dev, width)

    def ring(part):
        half = tok_dev // 2
        right, left = shift(part[5, :half].astype(BF), 1), shift(part[5, half:].astype(BF), -1)
        right = jnp.pad(right.astype(F32), ((0, half), (0, 0))) + part[4]
        left = jnp.pad(left.astype(F32), ((half, 0), (0, 0))) + part[3]
        return shift(right.astype(BF), 1), shift(left.astype(BF), -1)

    def onward(part, right, left):
        right, left = right.astype(F32) + part[2], left.astype(F32) + part[1]
        return shift(right.astype(BF), 1), shift(left.astype(BF), -1)

    far = gather_sums(far_mixed_matrix, ret_mixed, 6)
    ends = token_dots(ret_mixed, sent_grads[:, 8:], prob_far, slot_far - 8, hit_far)
    far = jnp.concatenate([far, ends.reshape(6, tok_dev, LANES)], axis=2)
    far_mixed = far
    mixed_right, mixed_left = ring(far)
    ret_back, mixed_right, mixed_left = lax.optimization_barrier(
        (ret_back, mixed_right, mixed_left)
    )

    mixed_right, mixed_left = onward(far_mixed, mixed_right, mixed_left)
    ret_back, back_near = lax.optimization_barrier((ret_back, back_near))
    ret_near = route(back_near)
    far = gather_sums(far_back_matrix, ret_back, 6)
    far_back = far
    back_right, back_left = onward(far, *ring(far))
    ret_near, back_right, back_left = lax.optimization_barrier((ret_near, back_right, back_left))

    sides = gather_sums(near_matrix, ret_near, 4)
    here = gather_sums(own_matrix, ret_near, 2)
    ends = token_dots(ret_near[:, :8], sent_grads[:, :8], prob_near, slot_near, hit_near)
    ends = ends.reshape(3, tok_dev, LANES)

    def beside(at, mixed, back):
        rows = sides[at - 1] + mixed[:, :width], sides[at + 1] + back
        return jnp.concatenate(rows + (ends[at] + mixed[:, width:],), axis=1)

    right = beside(
        2, mixed_right.astype(F32) + far_mixed[0], back_right.astype(F32) + far_back[0]
    )
    left = beside(1, mixed_left.astype(F32), back_left.astype(F32))
    total = shift(right.astype(BF), 1).astype(F32) + shift(left.astype(BF), -1).astype(F32)
    mixed = (total[:, :width] + here[0]).astype(BF)
    grad_tokens = (total[:, width : 2 * width] + here[1]).astype(BF)
    ends = total[:, 2 * width :] + ends[0]
    grad_probs = ends[:, :top] + ends[:, top : 2 * top] + ends[:, 2 * top : 3 * top]
    return (mixed, grad_tokens, grad_probs)


def solution(mesh):
    fine = Mesh(mesh.devices.reshape(4, 4, 8, 2), ("y", "x", "z", "core"))
    both = ("y", "x", "z", "core")
    return jax.shard_map(
        body,
        mesh=fine,
        in_specs=(
            P(both, None),
            P(both, None),
            P(both, None),
            P(both, None, None),
            P(both, None, None),
            P(both, None, None),
            P(both, None),
        ),
        out_specs=(P(both, None), P(both, None), P(both, None)),
        check_vma=False,
    )
```
